32 devices in a mesh: perm: 2 (over y), subj: 8 (over z, core), vert: 2 (over x).
Axes of the slice: x: 2, y: 2, z: 4, core: 2. Of those that a mesh axis runs over, the one named last changes fastest.
Arguments:
- kinship: bfloat16 [2048, 2048], P('subj')
- phenotype: bfloat16 [2048, 2048], P('subj', 'vert')
- shuffle: int32 [4096], P(('perm', 'subj')), parts along dimension 0, may hold values from 0 to 2047, as said below
Outputs:
- statistic: float32 [4096], P(('perm', 'vert')), parts along dimension 0
The draws below stay inside these ranges and needn't reach their ends.
There are 2 independent parts, one for each index of `perm`. The reference program is written for one: setup_inputs(seed, part) draws one part's arguments, and reference() takes and returns one part's arrays. A program takes and returns all parts, laid end to end along the dimension named above; an argument that names none is the same for every part. Nothing has to cross between parts.
Inputs may be any that keep to these rules, and one draw needn't show every extreme that they name: shuffle is a permutation of 0 to 2047 that maps every subject into its own exchangeability block.
All inputs are finite; a program needn't handle non-finite values.
Results may differ from the reference program's by a relative error of at most 0.0003.
Values may be sent and summed in bfloat16 or wider, within the bound.
No kernel may reach another device: no remote copies, remote signals or barrier semaphores. Data moves between devices by JAX's collectives and lax.ppermute only.
A program may use at most 128 MiB of HBM per device.

```python
import jax
import jax.numpy as jnp
from jax import lax

BLOCKS = 16
SUBJECTS = 2048
VERTICES = 2048


def draw_kinship(key, part):
    key_noise, key_diag = jax.random.split(key)
    entries = jax.random.normal(key_noise, (SUBJECTS, SUBJECTS), jnp.float32)
    symmetric = 0.4 * (entries + entries.T) / jnp.sqrt(2.0 * SUBJECTS)
    diagonal = 0.8 + 0.4 * jax.random.uniform(key_diag, (SUBJECTS,), jnp.float32)
    identity = jnp.eye(SUBJECTS, dtype=jnp.float32)
    return (symmetric * (1.0 - identity) + identity * diagonal[:, None]).astype(jnp.bfloat16)


def draw_phenotype(key, part):
    key_noise, key_rows, key_cols = jax.random.split(key, 3)
    entries = jax.random.normal(key_noise, (SUBJECTS, VERTICES), jnp.float32)
    position = jnp.arange(SUBJECTS, dtype=jnp.float32) / SUBJECTS
    row_scale = jnp.exp(1.0986123 * position + 2.3025851 * jax.random.uniform(key_rows, (SUBJECTS,), jnp.float32)) / 4.0
    col_scale = jnp.exp(2.3025851 * jax.random.uniform(key_cols, (VERTICES,), jnp.float32)) / 3.0
    return (entries * row_scale[:, None] * col_scale[None, :]).astype(jnp.bfloat16)


def draw_shuffle(key, part):
    key_block, key_rank = jax.random.split(key)
    block_ids = jax.random.randint(key_block, (SUBJECTS,), 0, BLOCKS).astype(jnp.int32)
    ranks = jax.random.permutation(key_rank, SUBJECTS).astype(jnp.int32)
    positions = jnp.arange(SUBJECTS, dtype=jnp.int32)
    source_order = jnp.argsort(block_ids * SUBJECTS + ranks, stable=True).astype(jnp.int32)
    target_order = jnp.argsort(block_ids * SUBJECTS + positions, stable=True).astype(jnp.int32)
    return jnp.zeros((SUBJECTS,), jnp.int32).at[target_order].set(source_order)


def setup_inputs(seed: int = 0, part: int = 0) -> dict:
    streams_of = jax.random.split(jax.random.key(seed), 4)
    part_splits = jax.random.split(jax.random.fold_in(streams_of[3], part), 4)
    kinship = draw_kinship(jax.random.fold_in(streams_of[3], 71), part)
    phenotype = draw_phenotype(jax.random.fold_in(streams_of[3], 71), part)
    shuffle = draw_shuffle(jax.random.fold_in(jax.random.fold_in(streams_of[3], part), 71), part)
    return dict(kinship=kinship, phenotype=phenotype, shuffle=shuffle)


def reference(kinship, phenotype, shuffle):
    permuted = jnp.take(phenotype, shuffle.astype(jnp.int32), axis=0)
    product = jnp.dot(kinship, permuted, preferred_element_type=jnp.float32)
    kin_diag = jnp.diagonal(kinship).astype(jnp.float32)
    moved = permuted.astype(jnp.float32)
    cross_term = lax.optimization_barrier(jnp.sum(moved * (product - kin_diag[:, None] * moved), axis=0))
    values = phenotype.astype(jnp.float32)
    squares = lax.optimization_barrier(jnp.sum(values * values, axis=0))
    subject_count = kinship.shape[0]
    return cross_term / (jnp.sqrt(jnp.float32(subject_count)) * (squares / subject_count + 1e-05))
```

```python
import functools

import jax
import jax.numpy as jnp
from jax import lax
from jax.experimental import pallas as pl
from jax.experimental.pallas import tpu as pltpu
from jax.sharding import PartitionSpec as P

BF16, F32, I32 = jnp.bfloat16, jnp.float32, jnp.int32
LANES = 128


def in_vmem(x):
    return pltpu.with_memory_space_constraint(x, pltpu.VMEM)


def call(body, out, *args, flops=0):
    whole = pl.BlockSpec(memory_space=pltpu.VMEM)
    outs = [pltpu.VMEM(shape, dtype) for shape, dtype in out]
    size = sum(a.size * a.dtype.itemsize for a in args)
    return pl.pallas_call(
        body,
        out_shape=outs,
        in_specs=[whole] * len(args),
        out_specs=[whole] * len(outs),
        compiler_params=pltpu.CompilerParams(vmem_limit_bytes=16 << 20),
        cost_estimate=pl.CostEstimate(
            flops=flops, bytes_accessed=size, transcendentals=0
        ),
    )(*[in_vmem(a) for a in args])


def column_of(row):
    return jnp.transpose(jnp.broadcast_to(row, (LANES, row.shape[1])))


def picker(high, low, block, rows):
    shape = high.shape
    lane = lax.broadcasted_iota(I32, shape, 1)
    one, zero = jnp.ones(shape, BF16), jnp.zeros(shape, BF16)
    number = jnp.full(shape, block, F32).astype(BF16)
    inside = jnp.where(high == number, low, jnp.full(shape, -1, BF16))
    tiles = [
        jnp.where(inside == (lane + t).astype(F32).astype(BF16), one, zero)
        for t in range(0, rows, LANES)
    ]
    return jnp.concatenate(tiles, axis=1)


def split(column, rows):
    high = lax.div(column, rows)
    low = column - high * rows
    return high.astype(F32).astype(BF16), low.astype(F32).astype(BF16)


def square_rows(ref):
    v = ref[...].astype(F32)
    return jnp.sum(v * v, axis=0, keepdims=True)


def clear_diagonal(kin_ref, out_ref):
    rows = kin_ref.shape[0]
    first = pl.multiple_of(lax.axis_index("subj") * rows, LANES)
    out_ref[...] = kin_ref[...]
    r = lax.broadcasted_iota(I32, (rows, rows), 0)
    c = lax.broadcasted_iota(I32, (rows, rows), 1)
    own = kin_ref[:, pl.ds(first, rows)].astype(F32)
    out_ref[:, pl.ds(first, rows)] = jnp.where(r == c, 0.0, own).astype(BF16)


def move_rows(sources, shuffle_ref, *refs):
    n = len(sources)
    chunks, moved_ref, squares_ref = refs[:n], refs[n], refs[n + 1]
    rows, me = chunks[0].shape[0], lax.axis_index("subj")
    blocks = [me ^ s for s in sources]

    def tile(t, carry):
        high, low = split(column_of(shuffle_ref[pl.ds(t, 1), :]), rows)
        total = jnp.zeros((rows, chunks[0].shape[1]), F32)
        for block, chunk in zip(blocks, chunks):
            total += jnp.dot(
                picker(high, low, block, rows), chunk[...], preferred_element_type=F32
            )
        moved_ref[pl.ds(pl.multiple_of(t * rows, LANES), rows), :] = total.astype(BF16)
        return carry

    lax.fori_loop(0, shuffle_ref.shape[0], tile, 0, unroll=4)
    squares_ref[...] = sum(square_rows(c) for c in chunks)


def finish(sources, perms, shuffle_ref, moved_ref, squares_ref, own_ref, sib_ref, *refs):
    n = len(sources)
    chunks, out_ref, full_ref = refs[:n], refs[n], refs[n + 1]
    rows, me = chunks[0].shape[0], lax.axis_index("subj")
    blocks = [me ^ s for s in sources]
    tiles = shuffle_ref.shape[0]

    def tile(t, carry):
        high, low = split(column_of(shuffle_ref[pl.ds(t, 1), :]), rows)
        here = pl.ds(pl.multiple_of(t * rows, LANES), rows)
        total = moved_ref[here, :].astype(F32)
        for block, chunk in zip(blocks, chunks):
            total += jnp.dot(
                picker(high, low, block, rows), chunk[...], preferred_element_type=F32
            )
        full_ref[here, :] = total.astype(BF16)
        return carry

    lax.fori_loop(0, tiles, tile, 0, unroll=4)
    squares = squares_ref[...] + sum(square_rows(c) for c in chunks)
    subjects = tiles // perms * rows
    halves = squares.shape[1] // LANES
    dests = out_ref.shape[0] // perms
    for p in range(perms):
        x = full_ref[p * subjects : (p + 1) * subjects, :]
        cross = jnp.zeros_like(squares)
        for kin, block in ((own_ref, me), (sib_ref, me ^ 1)):
            product = jnp.dot(kin[...], x, preferred_element_type=F32)
            first = pl.multiple_of(p * subjects + block * rows, LANES)
            mine = full_ref[pl.ds(first, rows), :].astype(F32)
            cross += jnp.sum(mine * product, axis=0, keepdims=True)
        lines = [cross[:, h * LANES : (h + 1) * LANES] for h in range(halves)]
        lines += [squares[:, h * LANES : (h + 1) * LANES] for h in range(halves)]
        lines += [jnp.zeros((8 - 2 * halves, LANES), F32)]
        block = jnp.concatenate(lines, axis=0)
        for d in range(dests):
            out_ref[p * dests + d] = block


def per_device(n_perm, n_subj, kinship, phenotype, shuffle):
    rows, subjects = kinship.shape
    width = phenotype.shape[1] // (2 * n_perm)
    me = lax.axis_index("subj")
    core = lax.rem(me, 2)
    first = lax.axis_index("perm") * 2

    def exchange(x, mask):
        return lax.ppermute(x, "subj", [(i, i ^ mask) for i in range(n_subj)])

    mine = lax.dynamic_slice_in_dim(phenotype, (first + core) * width, width, 1)
    others = lax.dynamic_slice_in_dim(phenotype, (first + 1 - core) * width, width, 1)
    received = exchange(others, 1)
    own_kin = call(clear_diagonal, [((rows, subjects), BF16)], kinship)[0]
    sib_kin = exchange(own_kin, 1)

    everyone = jnp.broadcast_to(shuffle[None], (n_perm * n_subj, rows))
    shuffles = lax.all_to_all(everyone, ("perm", "subj"), 0, 0, tiled=True)

    chunks = [(0, mine), (1, received)]
    step = n_subj // 2
    while step > 1:
        chunks += [(s ^ step, exchange(x, step)) for s, x in chunks]
        step //= 2

    early, late = chunks[:-2], chunks[-2:]
    macs = shuffles.size * rows * width
    moved, squares = call(
        functools.partial(move_rows, [s for s, _ in early]),
        [((n_perm * subjects, width), BF16), ((1, width), F32)],
        shuffles,
        *[x for _, x in early],
        flops=2 * macs * len(early),
    )
    dests = n_perm * n_subj
    sums, _ = call(
        functools.partial(finish, [s for s, _ in late], n_perm),
        [((dests, 8, LANES), F32), ((n_perm * subjects, width), BF16)],
        shuffles,
        moved,
        squares,
        own_kin,
        sib_kin,
        *[x for _, x in late],
        flops=2 * macs * len(late) + 4 * n_perm * rows * subjects * width,
    )
    sums = lax.all_to_all(sums, ("perm", "subj"), 0, 0, tiled=True)
    sums = sums.reshape(n_perm, n_subj // 2, 2, 8, LANES)
    lines = width // LANES
    cross = jnp.sum(sums[:, :, :, :lines], axis=1)
    squares = sums[:, 0, :, lines : 2 * lines]
    count = jnp.float32(subjects)
    result = cross / (jnp.sqrt(count) * (squares / subjects + 1e-05))
    return result.reshape(-1)


def solution(mesh):
    in_specs = (P("subj", None), P("subj", "vert"), P(("perm", "subj")))
    out_specs = P(("perm", "vert"))
    body = functools.partial(per_device, mesh.shape["perm"], mesh.shape["subj"])
    return jax.shard_map(
        body, mesh=mesh, in_specs=in_specs, out_specs=out_specs, check_vma=False
    )
```

```python
import functools

import jax
import jax.numpy as jnp
from jax import lax
from jax.experimental import pallas as pl
from jax.experimental.pallas import tpu as pltpu
from jax.sharding import PartitionSpec as P

BF16, F32, I32 = jnp.bfloat16, jnp.float32, jnp.int32
LANES = 128


def call(body, out, *args, flops=0, scratch=(), from_hbm=0):
    space = [pltpu.HBM if i < from_hbm else pltpu.VMEM for i in range(len(args))]
    outs = [pltpu.VMEM(shape, dtype) for shape, dtype in out]
    size = sum(a.size * a.dtype.itemsize for a in args)
    return pl.pallas_call(
        body,
        out_shape=outs,
        in_specs=[pl.BlockSpec(memory_space=s) for s in space],
        out_specs=[pl.BlockSpec(memory_space=pltpu.VMEM)] * len(outs),
        scratch_shapes=scratch,
        compiler_params=pltpu.CompilerParams(vmem_limit_bytes=24 << 20),
        cost_estimate=pl.CostEstimate(
            flops=flops, bytes_accessed=size, transcendentals=0
        ),
    )(*[pltpu.with_memory_space_constraint(a, s) for a, s in zip(args, space)])


def dot(a, b):
    return jnp.dot(a, b, preferred_element_type=F32)


def tile_of(index, rows):
    return pl.ds(pl.multiple_of(index * rows, LANES), rows)


def square_rows(ref):
    v = ref[...].astype(F32)
    return jnp.sum(v * v, axis=0, keepdims=True)


def cut(
    order, phen_ref, kin_ref, shuffle_ref, mine_ref, others_ref, own_ref, sib_ref,
    everyone_ref, all_ref, line_ref, sems,
):
    rows, width = mine_ref.shape
    me = lax.axis_index("subj")
    core, first = lax.rem(me, 2), lax.axis_index("perm") * 2
    copies = [
        pltpu.make_async_copy(
            phen_ref.at[:, tile_of(first + core, width)], mine_ref, sems.at[0]
        ),
        pltpu.make_async_copy(
            phen_ref.at[:, tile_of(first + 1 - core, width)], others_ref, sems.at[1]
        ),
        pltpu.make_async_copy(kin_ref, all_ref, sems.at[2]),
        pltpu.make_async_copy(shuffle_ref, line_ref, sems.at[3]),
    ]
    for copy in copies:
        copy.start()
    for copy in copies:
        copy.wait()
    everyone_ref[...] = jnp.broadcast_to(line_ref[...], everyone_ref.shape)
    r = lax.broadcasted_iota(I32, (rows, rows), 0)
    c = lax.broadcasted_iota(I32, (rows, rows), 1)
    for i, source in enumerate(order):
        block = all_ref[:, tile_of(me ^ source, rows)]
        if source == 0:
            block = jnp.where(r == c, 0.0, block.astype(F32)).astype(BF16)
        j = order.index(source ^ 1)
        own_ref[:, i * rows : (i + 1) * rows] = block
        sib_ref[:, j * rows : (j + 1) * rows] = block


def columns_of(shuffle_ref, row, rows):
    line = jnp.broadcast_to(shuffle_ref[row : row + 1, :], (LANES, rows))
    column = jnp.transpose(line)
    high = lax.div(column, rows)
    low = column - high * rows
    return high.astype(F32).astype(BF16), low.astype(F32).astype(BF16)


def picker(digits, block, rows):
    high, low = digits
    shape = high.shape
    lane = lax.broadcasted_iota(I32, shape, 1)
    one, zero = jnp.ones(shape, BF16), jnp.zeros(shape, BF16)
    number = jnp.full(shape, block, F32).astype(BF16)
    inside = jnp.where(high == number, low, jnp.full(shape, -1, BF16))
    tiles = [
        jnp.where(inside == (lane + t).astype(F32).astype(BF16), one, zero)
        for t in range(0, rows, LANES)
    ]
    return jnp.concatenate(tiles, axis=1)


def find(order, chunks, digits, rows):
    me = lax.axis_index("subj")
    parts = [dot(picker(digits, me ^ s, rows), c[...]) for s, c in zip(order, chunks)]
    return sum(parts).astype(BF16)


def line_of(ref, perm, subj, perms):
    return ref[pl.ds(perm * (ref.shape[0] // perms) + subj, 1), :]


def square(a_ref, b_ref, out_ref):
    out_ref[...] = square_rows(a_ref) + square_rows(b_ref)


def move(order, perms, shuffle_ref, some_ref, *refs):
    chunks, (moved_ref, squares_ref) = refs[:-2], refs[-2:]
    rows, me = chunks[0].shape[0], lax.axis_index("subj")
    n = len(order)
    for p in range(perms):
        for i in range(n):
            digits = columns_of(line_of(shuffle_ref, p, me ^ order[i], perms), 0, rows)
            at = (p * n + i) * rows
            moved_ref[at : at + rows, :] = find(order, chunks, digits, rows)
    squares_ref[...] = some_ref[...] + sum(square_rows(c) for c in chunks[2:])


def add_block(order, which, perms, shuffle_ref, moved_ref, squares_ref, chunk_ref, *refs):
    moved_out, squares_out = refs
    rows, me = chunk_ref.shape[0], lax.axis_index("subj")
    n = len(order)
    for p in range(perms):
        for i in range(n):
            digits = columns_of(line_of(shuffle_ref, p, me ^ order[i], perms), 0, rows)
            here = slice((p * n + i) * rows, (p * n + i + 1) * rows)
            found = find([order[which]], [chunk_ref], digits, rows)
            moved_out[here, :] = moved_ref[here, :] + found
    squares_out[...] = squares_ref[...] + square_rows(chunk_ref)


def finish(order, perms, shuffle_ref, moved_ref, squares_ref, own_ref, sib_ref, last_ref, *refs):
    out_ref, full_ref = refs
    rows, me = last_ref.shape[0], lax.axis_index("subj")
    n = len(order)
    squares = squares_ref[...] + square_rows(last_ref)
    halves = squares.shape[1] // LANES
    dests = out_ref.shape[0] // perms
    for p in range(perms):
        for i in range(n):
            digits = columns_of(line_of(shuffle_ref, p, me ^ order[i], perms), 0, rows)
            here = slice((p * n + i) * rows, (p * n + i + 1) * rows)
            found = find(order[-1:], [last_ref], digits, rows)
            full_ref[i * rows : (i + 1) * rows, :] = moved_ref[here, :] + found
        cross = jnp.zeros_like(squares)
        for g, kin in enumerate((own_ref, sib_ref)):
            product = dot(kin[...], full_ref[...])
            mine = full_ref[g * rows : (g + 1) * rows, :].astype(F32)
            cross += jnp.sum(mine * product, axis=0, keepdims=True)
        lines = [cross[:, h * LANES : (h + 1) * LANES] for h in range(halves)]
        lines += [squares[:, h * LANES : (h + 1) * LANES] for h in range(halves)]
        lines += [jnp.zeros((8 - 2 * halves, LANES), F32)]
        block = jnp.concatenate(lines, axis=0)
        for d in range(dests):
            out_ref[p * dests + d] = block


def per_device(n_perm, n_subj, kinship, phenotype, shuffle):
    rows, subjects = kinship.shape
    width = phenotype.shape[1] // (2 * n_perm)

    def exchange(x, mask):
        return lax.ppermute(x, "subj", [(i, i ^ mask) for i in range(n_subj)])

    order, step = [0, 1], n_subj // 2
    while step > 1:
        order = order + [s ^ step for s in order]
        step //= 2

    mine, others, own_kin, for_sib, everyone = call(
        functools.partial(cut, order),
        [((rows, width), BF16)] * 2
        + [((rows, subjects), BF16)] * 2
        + [((n_perm * n_subj, rows), I32)],
        phenotype,
        kinship,
        shuffle[None],
        from_hbm=3,
        scratch=[
            pltpu.VMEM((rows, subjects), BF16),
            pltpu.VMEM((1, rows), I32),
            pltpu.SemaphoreType.DMA((4,)),
        ],
    )
    received = exchange(others, 1)
    sib_kin = exchange(for_sib, 1)
    shuffles = lax.all_to_all(everyone, ("perm", "subj"), 0, 0, tiled=True)

    chunks, step = [mine, received], n_subj // 2
    while step > 1:
        chunks = chunks + [exchange(x, step) for x in chunks]
        step //= 2

    table = [((n_perm * subjects, width), BF16), ((1, width), F32)]
    unit = 2 * rows * rows * width
    tiles = n_perm * n_subj
    squares = call(square, [((1, width), F32)], mine, received)[0]
    moved, squares = call(
        functools.partial(move, order, n_perm),
        table,
        shuffles,
        squares,
        *chunks[:-2],
        flops=unit * tiles * (n_subj - 2),
    )
    moved, squares = call(
        functools.partial(add_block, order, -2, n_perm),
        table,
        shuffles,
        moved,
        squares,
        chunks[-2],
        flops=unit * tiles,
    )
    sums = call(
        functools.partial(finish, order, n_perm),
        [((tiles, 8, LANES), F32)],
        shuffles,
        moved,
        squares,
        own_kin,
        sib_kin,
        chunks[-1],
        flops=unit * tiles * 3,
        scratch=[pltpu.VMEM((subjects, width), BF16)],
    )[0]
    sums = lax.all_to_all(sums, ("perm", "subj"), 0, 0, tiled=True)
    sums = sums.reshape(n_perm, n_subj // 2, 2, 8, LANES)
    lines = width // LANES
    cross = jnp.sum(sums[:, :, :, :lines], axis=1)
    squares = sums[:, 0, :, lines : 2 * lines]
    count = jnp.float32(subjects)
    result = cross / (jnp.sqrt(count) * (squares / subjects + 1e-05))
    return result.reshape(-1)


def solution(mesh):
    in_specs = (P("subj", None), P("subj", "vert"), P(("perm", "subj")))
    out_specs = P(("perm", "vert"))
    body = functools.partial(per_device, mesh.shape["perm"], mesh.shape["subj"])
    return jax.shard_map(
        body, mesh=mesh, in_specs=in_specs, out_specs=out_specs, check_vma=False
    )
```

```python
import functools

import jax
import jax.numpy as jnp
from jax import lax
from jax.experimental import pallas as pl
from jax.experimental.pallas import tpu as pltpu
from jax.sharding import PartitionSpec as P

BF16, F32, I32 = jnp.bfloat16, jnp.float32, jnp.int32
LANES = 128


def after(x, *others):
    return lax.optimization_barrier((x, *others))[0]


def call(body, out, *args, flops=0, scratch=(), from_hbm=0, to_hbm=0):
    ins = [pltpu.HBM if i < from_hbm else pltpu.VMEM for i in range(len(args))]
    outs = [pltpu.HBM if i < to_hbm else pltpu.VMEM for i in range(len(out))]
    size = sum(a.size * a.dtype.itemsize for a in args)
    return pl.pallas_call(
        body,
        out_shape=[space(shape, dtype) for space, (shape, dtype) in zip(outs, out)],
        in_specs=[pl.BlockSpec(memory_space=space) for space in ins],
        out_specs=[pl.BlockSpec(memory_space=space) for space in outs],
        scratch_shapes=scratch,
        compiler_params=pltpu.CompilerParams(vmem_limit_bytes=24 << 20),
        cost_estimate=pl.CostEstimate(
            flops=flops, bytes_accessed=size, transcendentals=0
        ),
    )(*[pltpu.with_memory_space_constraint(a, s) for a, s in zip(args, ins)])


def dot(a, b):
    return jnp.dot(a, b, preferred_element_type=F32)


def tile_of(index, rows):
    return pl.ds(pl.multiple_of(index * rows, LANES), rows)


def square_rows(ref):
    v = ref[...].astype(F32)
    return jnp.sum(v * v, axis=0, keepdims=True)


def cut(phen_ref, shuffle_ref, everyone_ref, mine_ref, others_ref, line_ref, lines_ref, sems):
    width = mine_ref.shape[1]
    core, first = lax.rem(lax.axis_index("subj"), 2), lax.axis_index("perm") * 2
    copies = [
        pltpu.make_async_copy(shuffle_ref, line_ref, sems.at[0]),
        pltpu.make_async_copy(
            phen_ref.at[:, tile_of(first + core, width)], mine_ref, sems.at[1]
        ),
        pltpu.make_async_copy(
            phen_ref.at[:, tile_of(first + 1 - core, width)], others_ref, sems.at[2]
        ),
    ]
    for copy in copies:
        copy.start()
    copies[0].wait()
    for h in range(line_ref.shape[1] // LANES):
        piece = line_ref[:, h * LANES : (h + 1) * LANES]
        lines_ref[:, h, :] = jnp.broadcast_to(piece, (lines_ref.shape[0], LANES))
    send = pltpu.make_async_copy(lines_ref, everyone_ref, sems.at[3])
    send.start()
    for copy in copies[1:]:
        copy.wait()
    send.wait()


def clear(order, kin_ref, own_ref, *refs):
    sib_refs, (all_ref, sem) = refs[:-2], refs[-2:]
    rows, me = kin_ref.shape[0], lax.axis_index("subj")
    copy = pltpu.make_async_copy(kin_ref, all_ref, sem)
    copy.start()
    copy.wait()
    r = lax.broadcasted_iota(I32, (rows, rows), 0)
    c = lax.broadcasted_iota(I32, (rows, rows), 1)
    for i, source in enumerate(order):
        block = all_ref[:, tile_of(me ^ source, rows)]
        if source == 0:
            block = jnp.where(r == c, 0.0, block.astype(F32)).astype(BF16)
        own_ref[:, i * rows : (i + 1) * rows] = block
        at = order.index(source ^ 1) * rows
        for sib_ref in sib_refs:
            if 0 <= at < sib_ref.shape[1]:
                sib_ref[:, at : at + rows] = block
            at -= sib_ref.shape[1]


def columns_of(shuffle_ref, perm, subj, perms, rows):
    lines = shuffle_ref[perm * (shuffle_ref.shape[0] // perms) + subj]
    column = jnp.concatenate(
        [
            jnp.transpose(jnp.broadcast_to(lines[h : h + 1], (LANES, LANES)))
            for h in range(rows // LANES)
        ],
        axis=0,
    )
    high = lax.div(column, rows)
    low = column - high * rows
    return high.astype(F32).astype(BF16), low.astype(F32).astype(BF16)


def picker(digits, block, rows):
    high, low = digits
    shape = high.shape
    lane = lax.broadcasted_iota(I32, shape, 1)
    one, zero = jnp.ones(shape, BF16), jnp.zeros(shape, BF16)
    number = jnp.full(shape, block, F32).astype(BF16)
    inside = jnp.where(high == number, low, jnp.full(shape, -1, BF16))
    tiles = [
        jnp.where(inside == (lane + t).astype(F32).astype(BF16), one, zero)
        for t in range(0, rows, LANES)
    ]
    return jnp.concatenate(tiles, axis=1)


def find(order, chunks, digits, rows):
    me = lax.axis_index("subj")
    parts = [dot(picker(digits, me ^ s, rows), c[...]) for s, c in zip(order, chunks)]
    return sum(parts).astype(BF16)


def tile(index, rows):
    return slice(index * rows, (index + 1) * rows)


def times(parts, x):
    total, at = 0.0, 0
    for part in parts:
        total += dot(part[...], x[at : at + part.shape[1], :])
        at += part.shape[1]
    return total


def square(a_ref, b_ref, out_ref):
    out_ref[...] = square_rows(a_ref) + square_rows(b_ref)


def move(order, perms, shuffle_ref, some_ref, *refs):
    chunks, (moved_ref, squares_ref) = refs[:-2], refs[-2:]
    rows, me = chunks[0].shape[0], lax.axis_index("subj")
    n = len(order)
    for p in range(perms):
        for i in range(n):
            digits = columns_of(shuffle_ref, p, me ^ order[i], perms, rows)
            moved_ref[tile(p * n + i, rows), :] = find(order, chunks, digits, rows)
    squares_ref[...] = some_ref[...] + sum(square_rows(c) for c in chunks[2:])


def finish(order, perms, shuffle_ref, moved_ref, squares_ref, own_ref, last_ref, *refs):
    sib_refs, (out_ref, full_ref) = refs[:-2], refs[-2:]
    rows, me = last_ref.shape[0], lax.axis_index("subj")
    n = len(order)
    squares = squares_ref[...] + square_rows(last_ref)
    halves = squares.shape[1] // LANES
    dests = out_ref.shape[0] // perms
    for p in range(perms):
        for i in range(n):
            digits = columns_of(shuffle_ref, p, me ^ order[i], perms, rows)
            found = find(order[-1:], [last_ref], digits, rows)
            full_ref[tile(i, rows), :] = moved_ref[tile(p * n + i, rows), :] + found
        cross = jnp.zeros_like(squares)
        for g, product in enumerate([dot(own_ref[...], full_ref[...]), times(sib_refs, full_ref)]):
            mine = full_ref[tile(g, rows), :].astype(F32)
            cross += jnp.sum(mine * product, axis=0, keepdims=True)
        lines = [cross[:, h * LANES : (h + 1) * LANES] for h in range(halves)]
        lines += [squares[:, h * LANES : (h + 1) * LANES] for h in range(halves)]
        lines += [jnp.zeros((8 - 2 * halves, LANES), F32)]
        block = jnp.concatenate(lines, axis=0)
        for d in range(dests):
            out_ref[p * dests + d] = block


def per_device(n_perm, n_subj, kinship, phenotype, shuffle):
    rows, subjects = kinship.shape
    width = phenotype.shape[1] // (2 * n_perm)

    def exchange(x, mask):
        return lax.ppermute(x, "subj", [(i, i ^ mask) for i in range(n_subj)])

    order, step = [0, 1], n_subj // 2
    while step > 1:
        order = order + [s ^ step for s in order]
        step //= 2

    parts = [k * subjects // 8 for k in (3,3,2)]
    everyone, mine, others = call(
        cut,
        [
            ((n_perm * n_subj, 8, LANES), I32),
            ((rows, width), BF16),
            ((rows, width), BF16),
        ],
        phenotype,
        shuffle[None],
        from_hbm=2,
        to_hbm=1,
        scratch=[
            pltpu.VMEM((1, rows), I32),
            pltpu.VMEM((n_perm * n_subj, 8, LANES), I32),
            pltpu.SemaphoreType.DMA((4,)),
        ],
    )
    own_kin, *for_sib = call(
        functools.partial(clear, order),
        [((rows, subjects), BF16)] + [((rows, part), BF16) for part in parts],
        kinship,
        from_hbm=1,
        scratch=[pltpu.VMEM((rows, subjects), BF16), pltpu.SemaphoreType.DMA],
        flops=0,
    )
    received = exchange(others, 1)
    shuffles = lax.all_to_all(everyone, ("perm", "subj"), 0, 0, tiled=True)
    sib_kin = [
        exchange(x if k < 0 else after(x, shuffles), 1) for k, x in enumerate(for_sib)
    ]

    chunks, step = [mine, received], n_subj // 2
    while step > 1:
        chunks = chunks + [exchange(x, step) for x in chunks]
        step //= 2

    table = [((n_perm * subjects, width), BF16), ((1, width), F32)]
    unit = 2 * rows * rows * width
    tiles = n_perm * n_subj
    squares = call(square, [((1, width), F32)], mine, received)[0]
    moved, squares = call(
        functools.partial(move, order, n_perm),
        table,
        shuffles,
        squares,
        *chunks[:-1],
        flops=unit * tiles * (n_subj - 1),
    )
    sums = call(
        functools.partial(finish, order, n_perm),
        [((tiles, 8, LANES), F32)],
        shuffles,
        moved,
        squares,
        own_kin,
        chunks[-1],
        *sib_kin,
        flops=unit * tiles * 3,
        scratch=[pltpu.VMEM((subjects, width), BF16)],
    )[0]
    sums = lax.all_to_all(sums, ("perm", "subj"), 0, 0, tiled=True)
    sums = sums.reshape(n_perm, n_subj // 2, 2, 8, LANES)
    lines = width // LANES
    cross = jnp.sum(sums[:, :, :, :lines], axis=1)
    squares = sums[:, 0, :, lines : 2 * lines]
    count = jnp.float32(subjects)
    result = cross / (jnp.sqrt(count) * (squares / subjects + 1e-05))
    return result.reshape(-1)


def solution(mesh):
    in_specs = (P("subj", None), P("subj", "vert"), P(("perm", "subj")))
    out_specs = P(("perm", "vert"))
    body = functools.partial(per_device, mesh.shape["perm"], mesh.shape["subj"])
    return jax.shard_map(
        body, mesh=mesh, in_specs=in_specs, out_specs=out_specs, check_vma=False
    )
```

```python
import functools

import jax
import jax.numpy as jnp
from jax import lax
from jax.experimental import pallas as pl
from jax.experimental.pallas import tpu as pltpu
from jax.sharding import PartitionSpec as P

BF16, F32, I32 = jnp.bfloat16, jnp.float32, jnp.int32
LANES = 128


def after(x, *others):
    return lax.optimization_barrier((x, *others))[0]


def call(body, out, *args, flops=0, scratch=(), from_hbm=0, to_hbm=0, size=None):
    ins = [pltpu.HBM if i < from_hbm else pltpu.VMEM for i in range(len(args))]
    outs = [pltpu.HBM if i < to_hbm else pltpu.VMEM for i in range(len(out))]
    if size is None:
        size = sum(a.size * a.dtype.itemsize for a in args)
    return pl.pallas_call(
        body,
        out_shape=[space(shape, dtype) for space, (shape, dtype) in zip(outs, out)],
        in_specs=[pl.BlockSpec(memory_space=space) for space in ins],
        out_specs=[pl.BlockSpec(memory_space=space) for space in outs],
        scratch_shapes=scratch,
        compiler_params=pltpu.CompilerParams(vmem_limit_bytes=24 << 20),
        cost_estimate=pl.CostEstimate(
            flops=flops, bytes_accessed=size, transcendentals=0
        ),
    )(*[pltpu.with_memory_space_constraint(a, s) for a, s in zip(args, ins)])


def dot(a, b):
    return jnp.dot(a, b, preferred_element_type=F32)


def tile_of(index, rows):
    return pl.ds(pl.multiple_of(index * rows, LANES), rows)


def square_rows(ref):
    v = ref[...].astype(F32)
    return jnp.sum(v * v, axis=0, keepdims=True)


def cut(phen_ref, shuffle_ref, everyone_ref, mine_ref, others_ref, line_ref, lines_ref, sems):
    width = mine_ref.shape[1]
    core, first = lax.rem(lax.axis_index("subj"), 2), lax.axis_index("perm") * 2
    copies = [
        pltpu.make_async_copy(shuffle_ref, line_ref, sems.at[0]),
        pltpu.make_async_copy(
            phen_ref.at[:, tile_of(first + core, width)], mine_ref, sems.at[1]
        ),
        pltpu.make_async_copy(
            phen_ref.at[:, tile_of(first + 1 - core, width)], others_ref, sems.at[2]
        ),
    ]
    for copy in copies:
        copy.start()
    copies[0].wait()
    for h in range(line_ref.shape[1] // LANES):
        piece = line_ref[:, h * LANES : (h + 1) * LANES]
        lines_ref[:, h, :] = jnp.broadcast_to(piece, (lines_ref.shape[0], LANES))
    send = pltpu.make_async_copy(lines_ref, everyone_ref, sems.at[3])
    send.start()
    for copy in copies[1:]:
        copy.wait()
    send.wait()


def clear(order, kin_ref, own_ref, *refs):
    sib_refs, (all_ref, sem) = refs[:-2], refs[-2:]
    rows, me = kin_ref.shape[0], lax.axis_index("subj")
    copy = pltpu.make_async_copy(kin_ref, all_ref, sem)
    copy.start()
    copy.wait()
    r = lax.broadcasted_iota(I32, (rows, rows), 0)
    c = lax.broadcasted_iota(I32, (rows, rows), 1)
    for i, source in enumerate(order):
        block = all_ref[:, tile_of(me ^ source, rows)]
        if source == 0:
            block = jnp.where(r == c, 0.0, block.astype(F32)).astype(BF16)
        own_ref[:, i * rows : (i + 1) * rows] = block
        at = order.index(source ^ 1) * rows
        for sib_ref in sib_refs:
            if 0 <= at < sib_ref.shape[1]:
                sib_ref[:, at : at + rows] = block
            at -= sib_ref.shape[1]


def columns_of(shuffle_ref, perm, subj, perms, rows):
    lines = shuffle_ref[perm * (shuffle_ref.shape[0] // perms) + subj]
    column = jnp.concatenate(
        [
            jnp.transpose(jnp.broadcast_to(lines[h : h + 1], (LANES, LANES)))
            for h in range(rows // LANES)
        ],
        axis=0,
    )
    high = lax.div(column, rows)
    low = column - high * rows
    return high.astype(F32).astype(BF16), low.astype(F32).astype(BF16)


def picker(digits, block, rows):
    high, low = digits
    shape = high.shape
    lane = lax.broadcasted_iota(I32, shape, 1)
    one, zero = jnp.ones(shape, BF16), jnp.zeros(shape, BF16)
    number = jnp.full(shape, block, F32).astype(BF16)
    inside = jnp.where(high == number, low, jnp.full(shape, -1, BF16))
    tiles = [
        jnp.where(inside == (lane + t).astype(F32).astype(BF16), one, zero)
        for t in range(0, rows, LANES)
    ]
    return jnp.concatenate(tiles, axis=1)


def find(order, chunks, digits, rows):
    me = lax.axis_index("subj")
    parts = [dot(picker(digits, me ^ s, rows), c[...]) for s, c in zip(order, chunks)]
    return sum(parts).astype(BF16)


def tile(index, rows):
    return slice(index * rows, (index + 1) * rows)


def times(parts, x):
    total, at = 0.0, 0
    for part in parts:
        total += dot(part[...], x[at : at + part.shape[1], :])
        at += part.shape[1]
    return total


def move(order, perms, sources, shuffle_ref, *refs):
    n = len(order)
    chunks, before, (moved_ref, squares_ref) = refs[: len(sources)], refs[len(sources) : -2], refs[-2:]
    rows, me = chunks[0].shape[0], lax.axis_index("subj")
    for p in range(perms):
        for i in range(n):
            digits = columns_of(shuffle_ref, p, me ^ order[i], perms, rows)
            here = tile(p * n + i, rows)
            more = find(sources, chunks, digits, rows)
            moved_ref[here, :] = before[0][here, :] + more if before else more
    squares = sum(square_rows(c) for c in chunks)
    squares_ref[...] = before[1][...] + squares if before else squares


def finish(order, perms, shuffle_ref, moved_ref, squares_ref, own_ref, last_ref, *refs):
    sib_refs, (out_ref, full_ref) = refs[:-2], refs[-2:]
    rows, me = last_ref.shape[0], lax.axis_index("subj")
    n = len(order)
    squares = squares_ref[...] + square_rows(last_ref)
    halves = squares.shape[1] // LANES
    dests = out_ref.shape[0] // perms
    for p in range(perms):
        for i in range(n):
            digits = columns_of(shuffle_ref, p, me ^ order[i], perms, rows)
            found = find(order[-1:], [last_ref], digits, rows)
            full_ref[tile(i, rows), :] = moved_ref[tile(p * n + i, rows), :] + found
        cross = jnp.zeros_like(squares)
        for g, product in enumerate([dot(own_ref[...], full_ref[...]), times(sib_refs, full_ref)]):
            mine = full_ref[tile(g, rows), :].astype(F32)
            cross += jnp.sum(mine * product, axis=0, keepdims=True)
        lines = [cross[:, h * LANES : (h + 1) * LANES] for h in range(halves)]
        lines += [squares[:, h * LANES : (h + 1) * LANES] for h in range(halves)]
        lines += [jnp.zeros((8 - 2 * halves, LANES), F32)]
        block = jnp.concatenate(lines, axis=0)
        for d in range(dests):
            out_ref[p * dests + d] = block


def per_device(n_perm, n_subj, kinship, phenotype, shuffle):
    rows, subjects = kinship.shape
    width = phenotype.shape[1] // (2 * n_perm)

    def exchange(x, mask):
        return lax.ppermute(x, "subj", [(i, i ^ mask) for i in range(n_subj)])

    order, step = [0, 1], n_subj // 2
    while step > 1:
        order = order + [s ^ step for s in order]
        step //= 2

    parts = [k * subjects // 8 for k in (3,3,2)]
    everyone, mine, others = call(
        cut,
        [
            ((n_perm * n_subj, 8, LANES), I32),
            ((rows, width), BF16),
            ((rows, width), BF16),
        ],
        phenotype,
        shuffle[None],
        from_hbm=2,
        to_hbm=1,
        scratch=[
            pltpu.VMEM((1, rows), I32),
            pltpu.VMEM((n_perm * n_subj, 8, LANES), I32),
            pltpu.SemaphoreType.DMA((4,)),
        ],
    )
    own_kin, *for_sib = call(
        functools.partial(clear, order),
        [((rows, subjects), BF16)] + [((rows, part), BF16) for part in parts],
        kinship,
        from_hbm=1,
        scratch=[pltpu.VMEM((rows, subjects), BF16), pltpu.SemaphoreType.DMA],
        flops=0,
    )
    received = exchange(others, 1)
    shuffles = lax.all_to_all(everyone, ("perm", "subj"), 0, 0, tiled=True)
    sib_kin = [
        exchange(x if k < 0 else after(x, shuffles), 1) for k, x in enumerate(for_sib)
    ]

    chunks, step = [mine, received], n_subj // 2
    while step > 1:
        chunks = chunks + [exchange(x, step) for x in chunks]
        step //= 2

    table = [((n_perm * subjects, width), BF16), ((1, width), F32)]
    unit = 2 * rows * rows * width
    tiles = n_perm * n_subj
    half = n_subj // 2
    met = [0, 1, 2, half]
    late = [i for i in range(n_subj - 1) if i not in met]
    moved, squares = call(
        functools.partial(move, order, n_perm, [order[i] for i in met]),
        table,
        shuffles,
        *[chunks[i] for i in met],
        size=0,
    )
    moved, squares = call(
        functools.partial(move, order, n_perm, [order[i] for i in late]),
        table,
        shuffles,
        *[chunks[i] for i in late],
        moved,
        squares,
        flops=unit * tiles * (n_subj - 1),
    )
    sums = call(
        functools.partial(finish, order, n_perm),
        [((tiles, 8, LANES), F32)],
        shuffles,
        moved,
        squares,
        own_kin,
        chunks[-1],
        *sib_kin,
        flops=unit * tiles * 3,
        scratch=[pltpu.VMEM((subjects, width), BF16)],
    )[0]
    sums = lax.all_to_all(sums, ("perm", "subj"), 0, 0, tiled=True)
    sums = sums.reshape(n_perm, n_subj // 2, 2, 8, LANES)
    lines = width // LANES
    cross = jnp.sum(sums[:, :, :, :lines], axis=1)
    squares = sums[:, 0, :, lines : 2 * lines]
    count = jnp.float32(subjects)
    result = cross / (jnp.sqrt(count) * (squares / subjects + 1e-05))
    return result.reshape(-1)


def solution(mesh):
    in_specs = (P("subj", None), P("subj", "vert"), P(("perm", "subj")))
    out_specs = P(("perm", "vert"))
    body = functools.partial(per_device, mesh.shape["perm"], mesh.shape["subj"])
    return jax.shard_map(
        body, mesh=mesh, in_specs=in_specs, out_specs=out_specs, check_vma=False
    )
```

```python
import functools

import jax
import jax.numpy as jnp
from jax import lax
from jax.experimental import pallas as pl
from jax.experimental.pallas import tpu as pltpu
from jax.sharding import PartitionSpec as P

BF16, F32, I32 = jnp.bfloat16, jnp.float32, jnp.int32
LANES = 128


def after(x, *others):
    return lax.optimization_barrier((x, *others))[0]


def call(body, out, *args, flops=0, scratch=(), from_hbm=0, to_hbm=0, size=None):
    ins = [pltpu.HBM if i < from_hbm else pltpu.VMEM for i in range(len(args))]
    outs = [pltpu.HBM if i < to_hbm else pltpu.VMEM for i in range(len(out))]
    if size is None:
        size = sum(a.size * a.dtype.itemsize for a in args)
    return pl.pallas_call(
        body,
        out_shape=[space(shape, dtype) for space, (shape, dtype) in zip(outs, out)],
        in_specs=[pl.BlockSpec(memory_space=space) for space in ins],
        out_specs=[pl.BlockSpec(memory_space=space) for space in outs],
        scratch_shapes=scratch,
        compiler_params=pltpu.CompilerParams(vmem_limit_bytes=24 << 20),
        cost_estimate=pl.CostEstimate(
            flops=flops, bytes_accessed=size, transcendentals=0
        ),
    )(*[pltpu.with_memory_space_constraint(a, s) for a, s in zip(args, ins)])


def dot(a, b):
    return jnp.dot(a, b, preferred_element_type=F32)


def tile_of(index, rows):
    return pl.ds(pl.multiple_of(index * rows, LANES), rows)


def square_rows(ref):
    v = ref[...].astype(F32)
    return jnp.sum(v * v, axis=0, keepdims=True)


def cut(phen_ref, shuffle_ref, everyone_ref, mine_ref, others_ref, line_ref, lines_ref, sems):
    width = mine_ref.shape[1]
    core, first = lax.rem(lax.axis_index("subj"), 2), lax.axis_index("perm") * 2
    copies = [
        pltpu.make_async_copy(shuffle_ref, line_ref, sems.at[0]),
        pltpu.make_async_copy(
            phen_ref.at[:, tile_of(first + core, width)], mine_ref, sems.at[1]
        ),
        pltpu.make_async_copy(
            phen_ref.at[:, tile_of(first + 1 - core, width)], others_ref, sems.at[2]
        ),
    ]
    for copy in copies:
        copy.start()
    copies[0].wait()
    for h in range(line_ref.shape[1] // LANES):
        piece = line_ref[:, h * LANES : (h + 1) * LANES]
        lines_ref[:, h, :] = jnp.broadcast_to(piece, (lines_ref.shape[0], LANES))
    send = pltpu.make_async_copy(lines_ref, everyone_ref, sems.at[3])
    send.start()
    for copy in copies[1:]:
        copy.wait()
    send.wait()


def clear(order, kin_ref, own_ref, *refs):
    sib_refs, (all_ref, sem) = refs[:-2], refs[-2:]
    rows, me = kin_ref.shape[0], lax.axis_index("subj")
    copy = pltpu.make_async_copy(kin_ref, all_ref, sem)
    copy.start()
    copy.wait()
    r = lax.broadcasted_iota(I32, (rows, rows), 0)
    c = lax.broadcasted_iota(I32, (rows, rows), 1)
    for i, source in enumerate(order):
        block = all_ref[:, tile_of(me ^ source, rows)]
        if source == 0:
            block = jnp.where(r == c, 0.0, block.astype(F32)).astype(BF16)
        own_ref[:, i * rows : (i + 1) * rows] = block
        at = order.index(source ^ 1) * rows
        for sib_ref in sib_refs:
            if 0 <= at < sib_ref.shape[1]:
                sib_ref[:, at : at + rows] = block
            at -= sib_ref.shape[1]


def columns_of(shuffle_ref, perm, subj, perms, rows):
    lines = shuffle_ref[perm * (shuffle_ref.shape[0] // perms) + subj]
    column = jnp.concatenate(
        [
            jnp.transpose(jnp.broadcast_to(lines[h : h + 1], (LANES, LANES)))
            for h in range(rows // LANES)
        ],
        axis=0,
    )
    high = lax.div(column, rows)
    low = column - high * rows
    return high.astype(F32).astype(BF16), low.astype(F32).astype(BF16)


def picker(digits, block, rows):
    high, low = digits
    shape = high.shape
    lane = lax.broadcasted_iota(I32, shape, 1)
    one, zero = jnp.ones(shape, BF16), jnp.zeros(shape, BF16)
    number = jnp.full(shape, block, F32).astype(BF16)
    inside = jnp.where(high == number, low, jnp.full(shape, -1, BF16))
    tiles = [
        jnp.where(inside == (lane + t).astype(F32).astype(BF16), one, zero)
        for t in range(0, rows, LANES)
    ]
    return jnp.concatenate(tiles, axis=1)


def find(order, chunks, digits, rows):
    me = lax.axis_index("subj")
    parts = [dot(picker(digits, me ^ s, rows), c[...]) for s, c in zip(order, chunks)]
    return sum(parts).astype(BF16)


def tile(index, rows):
    return slice(index * rows, (index + 1) * rows)


def times(parts, x):
    total, at = 0.0, 0
    for part in parts:
        total += dot(part[...], x[at : at + part.shape[1], :])
        at += part.shape[1]
    return total


def move(order, perms, sources, shuffle_ref, *refs):
    n = len(order)
    chunks, before, (moved_ref, squares_ref) = refs[: len(sources)], refs[len(sources) : -2], refs[-2:]
    rows, me = chunks[0].shape[0], lax.axis_index("subj")
    for p in range(perms):
        for i in range(n):
            digits = columns_of(shuffle_ref, p, me ^ order[i], perms, rows)
            here = tile(p * n + i, rows)
            more = find(sources, chunks, digits, rows)
            moved_ref[here, :] = before[0][here, :] + more if before else more
    squares = sum(square_rows(c) for c in chunks)
    squares_ref[...] = before[1][...] + squares if before else squares


def weigh(order, perms, shuffle_ref, own_ref, weights_ref):
    rows, me = own_ref.shape[0], lax.axis_index("subj")
    for p in range(perms):
        picks = []
        for source in order:
            digits = columns_of(shuffle_ref, p, me ^ source, perms, rows)
            picks.append(picker(digits, me ^ order[-1], rows))
        picks = jnp.concatenate(picks, axis=0)
        weights_ref[tile(p, rows), :] = dot(own_ref[...], picks).astype(BF16)


def multiply(perms, moved_ref, own_ref, product_ref):
    rows = own_ref.shape[0]
    subjects = moved_ref.shape[0] // perms
    for p in range(perms):
        x = moved_ref[tile(p, subjects), :]
        product_ref[tile(p, rows), :] = dot(own_ref[...], x)


def finish(
    order, perms, shuffle_ref, moved_ref, squares_ref, weights_ref, product_ref, last_ref, *refs
):
    sib_refs, (out_ref, full_ref) = refs[:-2], refs[-2:]
    rows, me = last_ref.shape[0], lax.axis_index("subj")
    n = len(order)
    squares = squares_ref[...] + square_rows(last_ref)
    halves = squares.shape[1] // LANES
    dests = out_ref.shape[0] // perms
    for p in range(perms):
        for i in range(n):
            digits = columns_of(shuffle_ref, p, me ^ order[i], perms, rows)
            found = find(order[-1:], [last_ref], digits, rows)
            full_ref[tile(i, rows), :] = moved_ref[tile(p * n + i, rows), :] + found
        more = dot(weights_ref[tile(p, rows), :], last_ref[...])
        products = [product_ref[tile(p, rows), :] + more, times(sib_refs, full_ref)]
        cross = jnp.zeros_like(squares)
        for g, product in enumerate(products):
            mine = full_ref[tile(g, rows), :].astype(F32)
            cross += jnp.sum(mine * product, axis=0, keepdims=True)
        lines = [cross[:, h * LANES : (h + 1) * LANES] for h in range(halves)]
        lines += [squares[:, h * LANES : (h + 1) * LANES] for h in range(halves)]
        lines += [jnp.zeros((8 - 2 * halves, LANES), F32)]
        block = jnp.concatenate(lines, axis=0)
        for d in range(dests):
            out_ref[p * dests + d] = block


def per_device(n_perm, n_subj, kinship, phenotype, shuffle):
    rows, subjects = kinship.shape
    width = phenotype.shape[1] // (2 * n_perm)

    def exchange(x, mask):
        return lax.ppermute(x, "subj", [(i, i ^ mask) for i in range(n_subj)])

    order, step = [0, 1], n_subj // 2
    while step > 1:
        order = order + [s ^ step for s in order]
        step //= 2

    parts = [k * subjects // 8 for k in (3,3,2)]
    everyone, mine, others = call(
        cut,
        [
            ((n_perm * n_subj, 8, LANES), I32),
            ((rows, width), BF16),
            ((rows, width), BF16),
        ],
        phenotype,
        shuffle[None],
        from_hbm=2,
        to_hbm=1,
        scratch=[
            pltpu.VMEM((1, rows), I32),
            pltpu.VMEM((n_perm * n_subj, 8, LANES), I32),
            pltpu.SemaphoreType.DMA((4,)),
        ],
    )
    own_kin, *for_sib = call(
        functools.partial(clear, order),
        [((rows, subjects), BF16)] + [((rows, part), BF16) for part in parts],
        kinship,
        from_hbm=1,
        scratch=[pltpu.VMEM((rows, subjects), BF16), pltpu.SemaphoreType.DMA],
        flops=0,
    )
    received = exchange(others, 1)
    shuffles = lax.all_to_all(everyone, ("perm", "subj"), 0, 0, tiled=True)
    sib_kin = [
        exchange(x if k < 0 else after(x, shuffles), 1) for k, x in enumerate(for_sib)
    ]

    chunks, step = [mine, received], n_subj // 2
    while step > 1:
        chunks = chunks + [exchange(x, step) for x in chunks]
        step //= 2

    table = [((n_perm * subjects, width), BF16), ((1, width), F32)]
    unit = 2 * rows * rows * width
    tiles = n_perm * n_subj
    half = n_subj // 2
    met = [0, 1, 2, half]
    late = [i for i in range(n_subj - 1) if i not in met]
    moved, squares = call(
        functools.partial(move, order, n_perm, [order[i] for i in met]),
        table,
        shuffles,
        *[chunks[i] for i in met],
        size=0,
    )
    moved, squares = call(
        functools.partial(move, order, n_perm, [order[i] for i in late]),
        table,
        shuffles,
        *[chunks[i] for i in late],
        moved,
        squares,
        flops=unit * tiles * (n_subj - 1),
    )
    weights = call(
        functools.partial(weigh, order, n_perm),
        [((n_perm * rows, rows), BF16)],
        shuffles,
        own_kin,
        size=0,
    )[0]
    product = call(
        functools.partial(multiply, n_perm),
        [((n_perm * rows, width), F32)],
        moved,
        own_kin,
        size=0,
    )[0]
    sums = call(
        functools.partial(finish, order, n_perm),
        [((tiles, 8, LANES), F32)],
        shuffles,
        moved,
        squares,
        weights,
        product,
        chunks[-1],
        *sib_kin,
        flops=unit * tiles * 3,
        scratch=[pltpu.VMEM((subjects, width), BF16)],
    )[0]
    sums = lax.all_to_all(sums, ("perm", "subj"), 0, 0, tiled=True)
    sums = sums.reshape(n_perm, n_subj // 2, 2, 8, LANES)
    lines = width // LANES
    cross = jnp.sum(sums[:, :, :, :lines], axis=1)
    squares = sums[:, 0, :, lines : 2 * lines]
    count = jnp.float32(subjects)
    result = cross / (jnp.sqrt(count) * (squares / subjects + 1e-05))
    return result.reshape(-1)


def solution(mesh):
    in_specs = (P("subj", None), P("subj", "vert"), P(("perm", "subj")))
    out_specs = P(("perm", "vert"))
    body = functools.partial(per_device, mesh.shape["perm"], mesh.shape["subj"])
    return jax.shard_map(
        body, mesh=mesh, in_specs=in_specs, out_specs=out_specs, check_vma=False
    )
```
